128 devices in a mesh: dev: 128 (over z, y, x, core).
Axes of the slice: x: 4, y: 4, z: 4, core: 2. Of those that a mesh axis runs over, the one named last changes fastest.
Arguments:
- blocks: bfloat16 [8192, 128, 128], P('dev'), may hold values from -6 to 6
- row_maps: bfloat16 [8192, 128, 128], P('dev'), may hold values from -0.5 to 0.5
- col_maps: bfloat16 [8192, 128, 128], P('dev'), may hold values from -0.5 to 0.5
- targets: int32 [8192, 1], P('dev'), may hold values from 0 to 127; in each aligned block of 64 rows (0 to 63, 64 to 127, ...) at most 2 rows name the same one
- date_index: int32 [8192], P('dev'), may hold values from 0 to 31
Outputs:
- coefficients: float32 [896, 128, 128], P('dev')
- residuals: bfloat16 [8192, 128, 128], P('dev')
The draws below stay inside these ranges and needn't reach their ends.
Inputs may be any that keep to these rules, and one draw needn't show every extreme that they name: `targets`: among the 64 entries of one device no tile is named more than 2 times, a bound that some block reaches; every tile is named by some entry.
All inputs are finite; a program needn't handle non-finite values.
Results may differ from the reference program's by a relative error of at most 0.0049.
Values may be sent and summed in bfloat16 or wider, within the bound.
A program may use at most 64 MiB of HBM per device.

```python
import math
import jax
import jax.numpy as jnp
import numpy as np
from jax import lax

BLK = 128
DATES = 32
TERMS = 7
PIECES = 64
TILES = 128
CAP = 2
TOTAL = 8192
N_DEV = 128


def place_ends(values, rng, low, high):
    shape = values.shape
    place = [jax.random.randint(jax.random.fold_in(rng, axis), (), 0, shape[axis]) for axis in range(len(shape))]
    values = values.at[tuple(place)].set(low)
    longest = shape.index(max(shape))
    place[longest] = (place[longest] + 1) % shape[longest]
    return values.at[tuple(place)].set(high)


def steps_of(own_key, extent, cuts, smallest, largest):
    level = 1.0
    for axis_at, parts in cuts:
        heights = jax.random.uniform(jax.random.fold_in(jax.random.fold_in(own_key, 6), axis_at), (parts,), jnp.float32, smallest / len(cuts), largest / len(cuts))
        level = level * jnp.repeat(jnp.exp(heights), extent[axis_at] // parts).reshape((-1,) + (1,) * (len(extent) - 1 - axis_at))
    return level


def routed_block(key, own, number, rows, number_of, top, limit, lean):
    order = jax.random.permutation(key, number_of)
    crowded, common = shares(number_of, rows * top, limit, lean, True), shares(number_of, rows * top, limit, lean, False)
    places = jnp.arange(number_of)

    def named(lengths, offset_by):
        used = int((lengths > 0).sum())
        fixed = max(1, used // 4)
        moved = fixed + (places - fixed + offset_by * (used - fixed)) % max(1, number_of - fixed)
        return jnp.zeros((number_of,), jnp.int32).at[order[jnp.where(places < fixed, places, moved)]].set(jnp.asarray(lengths, jnp.int32))

    lengths = jnp.where(number % 4 == 0, named(crowded, number // 4), named(common, number - number // 4 - 1))
    mixed = jax.random.permutation(jax.random.fold_in(own, 3), number_of)
    source_of, receiver = mixed[0:number_of // 2 * 2:2], mixed[1:number_of // 2 * 2:2]
    room = jnp.minimum(lengths[source_of] - 1, limit - lengths[receiver]) // 2
    room = jnp.where((source_of == order[0]) | (receiver == order[0]) | (lengths[receiver] == 0), 0, jnp.maximum(room, 0))
    moved = jax.random.randint(jax.random.fold_in(own, 4), (number_of // 2,), 0, 1 << 20) % (room + 1)
    lengths = lengths.at[source_of].add(-moved).at[receiver].add(moved)
    members = jnp.searchsorted(jnp.cumsum(lengths), jnp.arange(rows * top), side="right").astype(jnp.int32)
    table = members.reshape(top, rows).T
    table = table[jax.random.permutation(jax.random.fold_in(own, 1), rows)]
    offset_by = jax.random.randint(jax.random.fold_in(own, 2), (rows, 1), 0, top)
    return jnp.take_along_axis(table, (jnp.arange(top)[None, :] + offset_by) % top, axis=1)


def shares(number_of, total, reach, lean, full):
    weights = [(1 << 20) // math.isqrt(standing ** lean) + 1 for standing in range(1, number_of + 1)]
    largest = reach if full else min(reach, max(-(-total // number_of), total * weights[0] // sum(weights)))
    least = 1 if total - largest >= number_of - 1 else 0
    holding, spare = [largest] + [least] * (number_of - 1), total - largest - least * (number_of - 1)
    while spare > 0:
        free = [i for i in range(1, number_of) if holding[i] < largest] or [i for i in range(1, number_of) if holding[i] < reach]
        pool, left = sum([weights[i] for i in free]), spare
        for i in free:
            addition = min(reach - holding[i], max(1, left * weights[i] // pool), spare)
            holding[i] = holding[i] + addition
            spare = spare - addition
    return np.array(holding)


def normal_values(key, extent, scale, reach, shards=(), kind=jnp.bfloat16):
    level = steps_of(key, extent, shards, -0.22, 0.18) if shards else 1.0
    values = jax.random.normal(key, extent, jnp.float32) * scale * level
    return jnp.minimum(jnp.maximum(values, -reach), reach).astype(kind)


def setup_inputs(seed: int = 0) -> dict:
    keys = jax.random.split(jax.random.key(seed), 6)
    blocks = normal_values(keys[0], (TOTAL, BLK, BLK), 1.0, 6.0, ((0, 128),))
    row_maps = normal_values(keys[1], (TOTAL, BLK, BLK), BLK ** -0.5, 0.5, ((0, 128),))
    col_maps = normal_values(keys[2], (TOTAL, BLK, BLK), BLK ** -0.5, 0.5, ((0, 128),))
    targets_keys = jax.random.split(jax.random.fold_in(keys[3], 1), TOTAL // PIECES)
    targets_turns = jax.random.permutation(jax.random.fold_in(keys[3], 3), TOTAL // PIECES)
    targets = jax.vmap(lambda own, number: routed_block(jax.random.fold_in(keys[3], 2), own, number, PIECES, TILES, 1, CAP, 2))(targets_keys, targets_turns).reshape((TOTAL, 1))
    date_index = place_ends(jax.random.randint(keys[4], (TOTAL,), 0, DATES), jax.random.fold_in(keys[4], 1), 0, DATES - 1).astype(jnp.int32)
    return {"blocks": blocks, "row_maps": row_maps, "col_maps": col_maps, "targets": targets, "date_index": date_index}


highest = lax.Precision.HIGHEST

def harmonic_table(length):
    angles = 2.0 * jnp.pi * jnp.arange(length, dtype=jnp.float32) / length
    columns = [jnp.ones_like(angles)]
    for degree in range(1, 4):
        columns.append(jnp.cos(degree * angles))
        columns.append(jnp.sin(degree * angles))
    return jnp.stack(columns, axis=1)

def forward_group(inputs):
    source, row_map, col_map = inputs
    half_step = jnp.einsum('pij,pkj->pik', source.astype(jnp.float32), col_map.astype(jnp.float32)).astype(jnp.bfloat16)
    return jnp.einsum('pij,pjk->pik', row_map.astype(jnp.float32), half_step.astype(jnp.float32)).astype(jnp.bfloat16)

def solve_one(factor, moment):
    return jax.scipy.linalg.cho_solve((factor, True), moment)

def reference(blocks, row_maps, col_maps, targets, date_index):
    harmonic = harmonic_table(DATES)
    piece_total = blocks.shape[0]
    grouped_blocks = blocks.reshape(N_DEV, PIECES, BLK, BLK)
    grouped_rows = row_maps.reshape(N_DEV, PIECES, BLK, BLK)
    grouped_cols = col_maps.reshape(N_DEV, PIECES, BLK, BLK)
    resampled = lax.map(forward_group, (grouped_blocks, grouped_rows, grouped_cols)).reshape(piece_total, BLK * BLK)
    tile_ids = targets[:, 0].astype(jnp.int32)
    cell_keys = tile_ids * DATES + date_index.astype(jnp.int32)
    observed = jax.ops.segment_sum(resampled.astype(jnp.float32), cell_keys, num_segments=N_DEV * DATES)
    tallies = jax.ops.segment_sum(jnp.ones((piece_total,), jnp.float32), cell_keys, num_segments=N_DEV * DATES).reshape(N_DEV, DATES)
    normal = jnp.einsum('dk,td,dl->tkl', harmonic, tallies, harmonic, precision=highest) + jnp.eye(harmonic.shape[1], dtype=jnp.float32)
    moments = jnp.einsum('dk,tdx->tkx', harmonic, observed.reshape(N_DEV, DATES, BLK * BLK), precision=highest)
    factors = jnp.linalg.cholesky(normal)
    coeffs = jax.vmap(solve_one)(factors, moments)

    def residual_group(inputs):
        source, row_map, col_map, tile_rows, stamps = inputs
        weights = harmonic[stamps]
        chosen = coeffs[tile_rows]
        predicted = jnp.einsum('sk,skx->sx', weights, chosen, precision=highest).astype(jnp.bfloat16).reshape(PIECES, BLK, BLK)
        half_step = jnp.einsum('pij,pjk->pik', predicted.astype(jnp.float32), col_map.astype(jnp.float32)).astype(jnp.bfloat16)
        adjoint = jnp.einsum('pji,pjk->pik', row_map.astype(jnp.float32), half_step.astype(jnp.float32))
        return (source.astype(jnp.float32) - adjoint).astype(jnp.bfloat16)
    residuals = lax.map(residual_group, (grouped_blocks, grouped_rows, grouped_cols, tile_ids.reshape(N_DEV, PIECES), date_index.astype(jnp.int32).reshape(N_DEV, PIECES)))
    coefficients = coeffs.reshape(N_DEV * TERMS, BLK, BLK)
    return (coefficients, residuals.reshape(piece_total, BLK, BLK))
```

```python
import functools

import jax
import jax.numpy as jnp
import numpy as np
from jax import lax
from jax.experimental import pallas as pl
from jax.experimental.pallas import tpu as pltpu
from jax.sharding import PartitionSpec as P

N = 128
DATES = 32
TERMS = 7
BLK = 128
UNIT = 16
UNITS = 4
PAIR = 256
LOW = 16
CHUNKS = ((0, 1), (1, 2), (3, 1))
MESH = pl.DeviceIdType.MESH
f32 = jnp.float32
bf16 = jnp.bfloat16
highest = lax.Precision.HIGHEST
PAIRS = [(k, l) for k in range(TERMS) for l in range(k + 1)]


def harmonic_table():
    angles = 2.0 * np.pi * np.arange(DATES) / DATES
    columns = [np.ones(DATES)]
    for degree in range(1, 4):
        columns.append(np.cos(degree * angles))
        columns.append(np.sin(degree * angles))
    return np.stack(columns, axis=1)


def iota(shape, dim):
    return lax.broadcasted_iota(jnp.int32, shape, dim)


def inverse_rows(normal):
    low = {}
    for j in range(TERMS):
        for i in range(j, TERMS):
            s = normal[i, j]
            for m in range(j):
                s = s - low[i, m] * low[j, m]
            if i == j:
                root = jnp.sqrt(s)
                low[j, j] = root
                low[j, "inv"] = 1.0 / root
            else:
                low[i, j] = s * low[j, "inv"]
    inv = {}
    for j in range(TERMS):
        inv[j, j] = low[j, "inv"]
        for i in range(j + 1, TERMS):
            s = low[i, j] * inv[j, j]
            for m in range(j + 1, i):
                s = s + low[i, m] * inv[m, j]
            inv[i, j] = -s * low[i, "inv"]
    out = []
    for k, l in PAIRS:
        s = inv[k, k] * inv[k, l]
        for m in range(k + 1, TERMS):
            s = s + inv[m, k] * inv[m, l]
        out.append(s)
    return out


def kernel(
    b_hbm, r_hbm, c_hbm, t_ref, d_ref, table_ref, products_ref,
    coef_hbm, res_hbm,
    bv, rv, cv, meta_own, meta, send1, recv1, send2, recv2, w, wt, tmp,
    trow, drow, tally, inv_rows, inv_full, moments, coefs, coef_send, coef_recv, ctmp, coef_out,
    load_sem, stage_sem, meta_ss, meta_rs, ss1, rs1, ss2, rs2, coef_ss, coef_rs, own_sem, out_sem,
):
    me = lax.axis_index("dev")
    loads = []
    for u in range(UNITS):
        part = pl.ds(u * UNIT, UNIT)
        loads.append([
            pltpu.make_async_copy(src.at[part], dst.at[part], load_sem.at[i, u])
            for i, (src, dst) in enumerate(((b_hbm, bv), (c_hbm, cv), (r_hbm, rv)))
        ])
    for group in loads:
        for copy in group:
            copy.start()

    barrier = pltpu.get_barrier_semaphore()
    base = (me // LOW) * LOW

    @pl.loop(1, LOW)
    def _(i):
        peer = base + lax.rem(me + i, LOW)
        pl.semaphore_signal(barrier, inc=1, device_id=(peer,), device_id_type=MESH)

    @pl.loop(1, N // LOW)
    def _(i):
        peer = lax.rem(me + i * LOW, N)
        pl.semaphore_signal(barrier, inc=1, device_id=(peer,), device_id_type=MESH)

    def resample(u):
        for copy in loads[u]:
            copy.wait()
        for e in range(UNIT):
            p = u * UNIT + e
            half = lax.dot_general(
                bv[p], cv[p], (((1,), (1,)), ((), ())), preferred_element_type=f32
            ).astype(bf16)
            tmp[pl.ds(e, BLK, stride=UNIT), :] = jnp.dot(rv[p], half, preferred_element_type=f32)

        @pl.loop(0, 8)
        def _(i):
            rows = tmp[pl.ds(pl.multiple_of(i * 256, 256), 256), :]
            send1[u, pl.ds(i * 16, 16)] = rows.astype(bf16).reshape(16, UNIT, BLK)

    def exchange(src, dst, ss, rs, first, count, lane):
        units = pl.ds(first, count)
        own = pltpu.make_async_copy(src.at[units, me], dst.at[units, me], own_sem.at[lane])
        own.start()

        @pl.loop(1, N)
        def _(i):
            peer = lax.rem(me + i, N)
            pltpu.make_async_remote_copy(
                src_ref=src.at[units, peer], dst_ref=dst.at[units, me],
                send_sem=ss, recv_sem=rs, device_id=(peer,), device_id_type=MESH,
            ).start()

        return own

    def settle(ref, sem, first, count):
        part = ref.at[pl.ds(first, count), pl.ds(0, N - 1)]
        pltpu.make_async_copy(part, part, sem).wait()

    meta_own[0:1, 0:64] = t_ref[...]
    meta_own[0:1, 64:128] = d_ref[...]
    resample(0)
    pl.semaphore_wait(barrier, LOW - 1 + N // LOW - 1)

    @pl.loop(1, N // LOW)
    def _(i):
        peer = lax.rem(me + i * LOW, N)
        pl.semaphore_signal(stage_sem, inc=1, device_id=(peer,), device_id_type=MESH)

    pl.semaphore_wait(stage_sem, N // LOW - 1)

    own_meta = pltpu.make_async_copy(meta_own, meta.at[me], own_sem.at[6])
    own_meta.start()

    @pl.loop(1, N)
    def _(i):
        peer = lax.rem(me + i, N)
        pltpu.make_async_remote_copy(
            src_ref=meta_own, dst_ref=meta.at[me],
            send_sem=meta_ss, recv_sem=meta_rs, device_id=(peer,), device_id_type=MESH,
        ).start()

    owns1 = []
    for c, (first, count) in enumerate(CHUNKS):
        for u in range(first, first + count):
            if u > 0:
                resample(u)
        owns1.append(exchange(send1, recv1, ss1.at[c], rs1.at[c], first, count, c))

    part = meta.at[pl.ds(0, N - 1)]
    pltpu.make_async_copy(part, part, meta_rs).wait()
    own_meta.wait()
    names = meta[:, 0, :].astype(f32).astype(bf16)
    lane_in, lane_out = iota((N, PAIR), 0), iota((N, PAIR), 1)
    mine = (lane_out // UNIT) == lax.rem(lane_in, 16)
    gather = (iota((8, N), 0) == iota((8, N), 1) // 16).astype(f32).astype(bf16)
    for u in range(UNITS):
        for start, out in ((0, trow), (64, drow)):
            pick = (lane_in == start + u * UNIT + lax.rem(lane_out, UNIT)).astype(f32).astype(bf16)
            spread = jnp.dot(names, pick, preferred_element_type=f32)
            spread = jnp.where(mine, spread, 0.0).astype(bf16)
            out[pl.ds(u * 8, 8), :] = jnp.dot(gather, spread, preferred_element_type=f32)

    tally[...] = jnp.zeros_like(tally)
    table = table_ref[...].astype(bf16)

    @pl.loop(0, UNITS)
    def _(u):
        @pl.loop(0, 8)
        def _(g):
            pair = u * 8 + g
            tile = trow[pl.ds(pair, 1), :]
            date = drow[pl.ds(pair, 1), :]
            tile_hot = (iota((N, PAIR), 0).astype(f32) == tile).astype(f32).astype(bf16)
            date_hot = (iota((DATES, PAIR), 0).astype(f32) == date).astype(f32).astype(bf16)
            tally[...] += lax.dot_general(
                date_hot, tile_hot, (((1,), (1,)), ((), ())), preferred_element_type=f32
            )
            weights = jnp.dot(table, date_hot, preferred_element_type=f32)
            lanes = pl.ds(pl.multiple_of(g * PAIR, PAIR), PAIR)
            for k in range(TERMS):
                w[u, pl.ds(k * N, N), lanes] = tile_hot * weights[k : k + 1, :].astype(bf16)
            columns = jnp.where(iota((8, PAIR), 0) == 7, tile, weights).T
            hit = iota((PAIR, N), 1).astype(f32) == columns[:, 7:8]
            for k in range(TERMS):
                wt[pair, :, pl.ds(k * N, N)] = jnp.where(hit, columns[:, k : k + 1], 0.0).astype(bf16)

    normal_rows = jnp.dot(products_ref[...], tally[...], precision=highest, preferred_element_type=f32)
    normal = {}
    for i, (k, l) in enumerate(PAIRS):
        row = normal_rows[i : i + 1, :]
        normal[k, l] = row + 1.0 if k == l else row
    inv_rows[...] = jnp.zeros_like(inv_rows)
    for i, row in enumerate(inverse_rows(normal)):
        inv_rows[i : i + 1, :] = row
    columns = inv_rows[...].T
    for i in range(len(PAIRS)):
        inv_full[i] = jnp.broadcast_to(columns[:, i : i + 1], (N, BLK))

    @pl.loop(0, UNITS * UNIT)
    def _(p):
        rv[p] = rv[p].T

    for c, (first, count) in enumerate(CHUNKS):
        settle(recv1, rs1.at[c], first, count)
        owns1[c].wait()
        for u in range(first, first + count):
            part = jnp.dot(
                w[u], recv1[u].reshape(N * UNIT, BLK), preferred_element_type=f32
            )
            if u == 0:
                moments[...] = part
            else:
                moments[...] += part

    at = {}
    for i, (k, l) in enumerate(PAIRS):
        at[k, l] = at[l, k] = i

    @pl.loop(0, N // 16)
    def _(i):
        rows = pl.multiple_of(i * 16, 16)
        given = [moments[pl.ds(l * N + rows, 16), :] for l in range(TERMS)]
        for k in range(TERMS):
            value = inv_full[at[k, 0], pl.ds(rows, 16), :] * given[0]
            for l in range(1, TERMS):
                value = value + inv_full[at[k, l], pl.ds(rows, 16), :] * given[l]
            coefs[pl.ds(k * N + rows, 16), :] = value.astype(bf16)
            ctmp[pl.ds(rows * 8 + k, 16, stride=8), :] = value
        ctmp[pl.ds(rows * 8 + 7, 16, stride=8), :] = jnp.zeros((16, BLK), f32)
        coef_send[pl.ds(rows, 16)] = (
            ctmp[pl.ds(rows * 8, 128), :].astype(bf16).reshape(16, 8, BLK)
        )

    own_coef = pltpu.make_async_copy(coef_send.at[me], coef_recv.at[me], own_sem.at[7])
    own_coef.start()

    @pl.loop(1, N)
    def _(i):
        peer = lax.rem(me + i, N)
        pltpu.make_async_remote_copy(
            src_ref=coef_send.at[peer], dst_ref=coef_recv.at[me],
            send_sem=coef_ss, recv_sem=coef_rs, device_id=(peer,), device_id_type=MESH,
        ).start()

    def predict(u):
        @pl.loop(0, 2)
        def _(i):
            rows = wt[pl.ds(u * 8 + i * 4, 4)].reshape(4 * PAIR, TERMS * N)
            value = jnp.dot(rows, coefs[...], preferred_element_type=f32)
            send2[u, pl.ds(i * 64, 64)] = value.astype(bf16).reshape(64, UNIT, BLK)

    owns2 = []
    for c, (first, count) in enumerate(CHUNKS):
        for u in range(first, first + count):
            predict(u)
        owns2.append(exchange(send2, recv2, ss2.at[c], rs2.at[c], first, count, 3 + c))

    part = coef_recv.at[pl.ds(0, N - 1)]
    pltpu.make_async_copy(part, part, coef_rs).wait()
    own_coef.wait()
    ctmp[...] = coef_recv[...].astype(f32).reshape(N * 8, BLK)
    for k in range(TERMS):
        coef_out[k] = ctmp[pl.ds(k, N, stride=8), :]
    outs = [pltpu.make_async_copy(coef_out, coef_hbm, out_sem.at[UNITS])]
    outs[0].start()

    for c, (first, count) in enumerate(CHUNKS):
        settle(recv2, rs2.at[c], first, count)
        owns2[c].wait()
        for u in range(first, first + count):
            @pl.loop(0, 8)
            def _(i):
                rows = recv2[u, pl.ds(i * 16, 16)].astype(f32).reshape(256, BLK)
                tmp[pl.ds(pl.multiple_of(i * 256, 256), 256), :] = rows

            for e in range(UNIT):
                p = u * UNIT + e
                predicted = tmp[pl.ds(e, BLK, stride=UNIT), :].astype(bf16)
                back = jnp.dot(predicted, cv[p], preferred_element_type=f32).astype(bf16)
                adjoint = jnp.dot(rv[p], back, preferred_element_type=f32)
                bv[p] = (bv[p].astype(f32) - adjoint).astype(bf16)
            part = pl.ds(u * UNIT, UNIT)
            outs.append(pltpu.make_async_copy(bv.at[part], res_hbm.at[part], out_sem.at[u]))
            outs[-1].start()

    part = meta.at[pl.ds(0, N - 1)]
    pltpu.make_async_copy(part, part, meta_ss).wait()
    part = coef_send.at[pl.ds(0, N - 1)]
    pltpu.make_async_copy(part, part, coef_ss).wait()
    for c, (first, count) in enumerate(CHUNKS):
        settle(send1, ss1.at[c], first, count)
        settle(send2, ss2.at[c], first, count)
    for copy in outs:
        copy.wait()


def on_device(blocks, row_maps, col_maps, targets, date_index):
    entries = UNITS * UNIT
    harmonic = harmonic_table()
    table = np.zeros((8, DATES), np.float32)
    table[:TERMS] = harmonic.T
    products = np.zeros((32, DATES), np.float32)
    for i, (k, l) in enumerate(PAIRS):
        products[i] = harmonic[:, k] * harmonic[:, l]
    dma = pltpu.SemaphoreType.DMA
    chunks = len(CHUNKS)
    vmem = pl.BlockSpec(memory_space=pltpu.VMEM)
    hbm = pl.BlockSpec(memory_space=pl.ANY)
    return pl.pallas_call(
        kernel,
        out_shape=(
            jax.ShapeDtypeStruct((TERMS, BLK, BLK), f32),
            jax.ShapeDtypeStruct((entries, BLK, BLK), bf16),
        ),
        in_specs=[hbm] * 3 + [vmem] * 4,
        out_specs=(hbm, hbm),
        scratch_shapes=[
            pltpu.VMEM((entries, BLK, BLK), bf16),
            pltpu.VMEM((entries, BLK, BLK), bf16),
            pltpu.VMEM((entries, BLK, BLK), bf16),
            pltpu.VMEM((1, 128), jnp.int32),
            pltpu.VMEM((N, 1, 128), jnp.int32),
            pltpu.VMEM((UNITS, N, UNIT, BLK), bf16),
            pltpu.VMEM((UNITS, N, UNIT, BLK), bf16),
            pltpu.VMEM((UNITS, N, UNIT, BLK), bf16),
            pltpu.VMEM((UNITS, N, UNIT, BLK), bf16),
            pltpu.VMEM((UNITS, TERMS * N, N * UNIT), bf16),
            pltpu.VMEM((UNITS * 8, PAIR, TERMS * N), bf16),
            pltpu.VMEM((N * UNIT, BLK), f32),
            pltpu.VMEM((UNITS * 8, PAIR), f32),
            pltpu.VMEM((UNITS * 8, PAIR), f32),
            pltpu.VMEM((DATES, N), f32),
            pltpu.VMEM((32, N), f32),
            pltpu.VMEM((len(PAIRS), N, BLK), f32),
            pltpu.VMEM((TERMS * N, BLK), f32),
            pltpu.VMEM((TERMS * N, BLK), bf16),
            pltpu.VMEM((N, 8, BLK), bf16),
            pltpu.VMEM((N, 8, BLK), bf16),
            pltpu.VMEM((N * 8, BLK), f32),
            pltpu.VMEM((TERMS, N, BLK), f32),
            dma((3, UNITS)),
            pltpu.SemaphoreType.REGULAR,
            dma,
            dma,
            dma((chunks,)),
            dma((chunks,)),
            dma((chunks,)),
            dma((chunks,)),
            dma,
            dma,
            dma((8,)),
            dma((UNITS + 1,)),
        ],
        compiler_params=pltpu.CompilerParams(
            collective_id=0, has_side_effects=True, vmem_limit_bytes=58 * 2**20
        ),
        name="fit",
    )(
        blocks, row_maps, col_maps, targets.reshape(1, entries), date_index.reshape(1, entries),
        jnp.asarray(table), jnp.asarray(products),
    )


def solution(mesh):
    placed = (
        P("dev", None, None),
        P("dev", None, None),
        P("dev", None, None),
        P("dev", None),
        P("dev"),
    )
    return jax.shard_map(
        on_device,
        mesh=mesh,
        in_specs=placed,
        out_specs=(P("dev", None, None), P("dev", None, None)),
        check_vma=False,
    )
```

```python
import functools

import jax
import jax.numpy as jnp
import numpy as np
from jax import lax
from jax.experimental import pallas as pl
from jax.experimental.pallas import tpu as pltpu
from jax.sharding import PartitionSpec as P

N = 128
DATES = 32
TERMS = 7
BLK = 128
UNIT = 16
UNITS = 4
PAIR = 256
LOW = 16
MOVES = 8
CHUNKS = ((0, 1), (1, 2), (3, 1))
MESH = pl.DeviceIdType.MESH
f32 = jnp.float32
bf16 = jnp.bfloat16
highest = lax.Precision.HIGHEST
PAIRS = [(k, l) for k in range(TERMS) for l in range(k + 1)]


def harmonic_table():
    angles = 2.0 * np.pi * np.arange(DATES) / DATES
    columns = [np.ones(DATES)]
    for degree in range(1, 4):
        columns.append(np.cos(degree * angles))
        columns.append(np.sin(degree * angles))
    return np.stack(columns, axis=1)


def iota(shape, dim):
    return lax.broadcasted_iota(jnp.int32, shape, dim)


def inverse_rows(normal):
    low = {}
    for j in range(TERMS):
        for i in range(j, TERMS):
            s = normal[i, j]
            for m in range(j):
                s = s - low[i, m] * low[j, m]
            if i == j:
                root = jnp.sqrt(s)
                low[j, j] = root
                low[j, "inv"] = 1.0 / root
            else:
                low[i, j] = s * low[j, "inv"]
    inv = {}
    for j in range(TERMS):
        inv[j, j] = low[j, "inv"]
        for i in range(j + 1, TERMS):
            s = low[i, j] * inv[j, j]
            for m in range(j + 1, i):
                s = s + low[i, m] * inv[m, j]
            inv[i, j] = -s * low[i, "inv"]
    out = []
    for k, l in PAIRS:
        s = inv[k, k] * inv[k, l]
        for m in range(k + 1, TERMS):
            s = s + inv[m, k] * inv[m, l]
        out.append(s)
    return out


def kernel(
    b_hbm, r_hbm, c_hbm, t_ref, d_ref, table_ref, products_ref,
    coef_hbm, res_hbm,
    bv, rv, cv, meta_own, meta, send1, recv1, send2, recv2, w, tmp,
    trow, drow, tally, inv_rows, inv_full, moments, coefs_t, coefs, coef_send, coef_recv, ctmp, coef_out,
    load_sem, stage_sem, meta_ss, meta_rs, ss1, rs1, ss2, rs2, coef_ss, coef_rs, own_sem, out_sem,
):
    me = lax.axis_index("dev")
    loads = []
    for u in range(UNITS):
        part = pl.ds(u * UNIT, UNIT)
        loads.append([
            pltpu.make_async_copy(src.at[part], dst.at[part], load_sem.at[i, u])
            for i, (src, dst) in enumerate(((b_hbm, bv), (c_hbm, cv), (r_hbm, rv)))
        ])
    for group in loads:
        for copy in group:
            copy.start()

    barrier = pltpu.get_barrier_semaphore()
    base = (me // LOW) * LOW

    @pl.loop(1, LOW)
    def _(i):
        peer = base + lax.rem(me + i, LOW)
        pl.semaphore_signal(barrier, inc=1, device_id=(peer,), device_id_type=MESH)

    @pl.loop(1, N // LOW)
    def _(i):
        peer = lax.rem(me + i * LOW, N)
        pl.semaphore_signal(barrier, inc=1, device_id=(peer,), device_id_type=MESH)

    def resample(u):
        for copy in loads[u]:
            copy.wait()
        for e in range(UNIT):
            p = u * UNIT + e
            half = lax.dot_general(
                bv[p], cv[p], (((1,), (1,)), ((), ())), preferred_element_type=f32
            ).astype(bf16)
            tmp[pl.ds(e, BLK, stride=UNIT), :] = jnp.dot(rv[p], half, preferred_element_type=f32)

        @pl.loop(0, 8)
        def _(i):
            rows = tmp[pl.ds(pl.multiple_of(i * 256, 256), 256), :]
            send1[u, pl.ds(i * 16, 16)] = rows.astype(bf16).reshape(16, UNIT, BLK)

    def exchange(src, dst, ss, rs, first, count, lane):
        units = pl.ds(first, count)
        own = pltpu.make_async_copy(src.at[units, me], dst.at[units, me], own_sem.at[lane])
        own.start()

        @pl.loop(1, N, unroll=4)
        def _(i):
            peer = lax.rem(me + i * 37, N)
            pltpu.make_async_remote_copy(
                src_ref=src.at[units, peer], dst_ref=dst.at[units, me],
                send_sem=ss, recv_sem=rs, device_id=(peer,), device_id_type=MESH,
            ).start()

        return own

    def settle(ref, sem, first, count):
        part = ref.at[pl.ds(first, count), pl.ds(0, N - 1)]
        pltpu.make_async_copy(part, part, sem).wait()

    meta_own[0:1, 0:64] = t_ref[...]
    meta_own[0:1, 64:128] = d_ref[...]
    resample(0)
    pl.semaphore_wait(barrier, LOW - 1 + N // LOW - 1)

    @pl.loop(1, N // LOW)
    def _(i):
        peer = lax.rem(me + i * LOW, N)
        pl.semaphore_signal(stage_sem, inc=1, device_id=(peer,), device_id_type=MESH)

    pl.semaphore_wait(stage_sem, N // LOW - 1)

    owns1 = []
    for c, (first, count) in enumerate(CHUNKS):
        for u in range(first, first + count):
            if u > 0:
                resample(u)
        owns1.append(exchange(send1, recv1, ss1.at[c], rs1.at[c], first, count, c))
        if c == 0:
            own_meta = pltpu.make_async_copy(meta_own, meta.at[me], own_sem.at[6])
            own_meta.start()

            @pl.loop(1, N, unroll=4)
            def _(i):
                peer = lax.rem(me + i * 37, N)
                pltpu.make_async_remote_copy(
                    src_ref=meta_own, dst_ref=meta.at[me],
                    send_sem=meta_ss, recv_sem=meta_rs, device_id=(peer,), device_id_type=MESH,
                ).start()

    part = meta.at[pl.ds(0, N - 1)]
    pltpu.make_async_copy(part, part, meta_rs).wait()
    own_meta.wait()
    names = meta[:, 0, :].astype(f32).astype(bf16)
    lane_in, lane_out = iota((N, PAIR), 0), iota((N, PAIR), 1)
    mine = (lane_out // UNIT) == lax.rem(lane_in, 16)
    gather = (iota((8, N), 0) == iota((8, N), 1) // 16).astype(f32).astype(bf16)
    for u in range(UNITS):
        for start, out in ((0, trow), (64, drow)):
            pick = (lane_in == start + u * UNIT + lax.rem(lane_out, UNIT)).astype(f32).astype(bf16)
            spread = jnp.dot(names, pick, preferred_element_type=f32)
            spread = jnp.where(mine, spread, 0.0).astype(bf16)
            out[pl.ds(u * 8, 8), :] = jnp.dot(gather, spread, preferred_element_type=f32)

    tally[...] = jnp.zeros_like(tally)
    table = table_ref[...].astype(bf16)

    @pl.loop(0, UNITS)
    def _(u):
        @pl.loop(0, 8)
        def _(g):
            pair = u * 8 + g
            tile = trow[pl.ds(pair, 1), :]
            date = drow[pl.ds(pair, 1), :]
            tile_hot = (iota((N, PAIR), 0).astype(f32) == tile).astype(f32).astype(bf16)
            date_hot = (iota((DATES, PAIR), 0).astype(f32) == date).astype(f32).astype(bf16)
            tally[...] += lax.dot_general(
                date_hot, tile_hot, (((1,), (1,)), ((), ())), preferred_element_type=f32
            )
            weights = jnp.dot(table, date_hot, preferred_element_type=f32)
            lanes = pl.ds(pl.multiple_of(g * PAIR, PAIR), PAIR)
            for k in range(TERMS):
                w[u, pl.ds(k * N, N), lanes] = tile_hot * weights[k : k + 1, :].astype(bf16)

    normal_rows = jnp.dot(products_ref[...], tally[...], precision=highest, preferred_element_type=f32)
    normal = {}
    for i, (k, l) in enumerate(PAIRS):
        row = normal_rows[i : i + 1, :]
        normal[k, l] = row + 1.0 if k == l else row
    inv_rows[...] = jnp.zeros_like(inv_rows)
    for i, row in enumerate(inverse_rows(normal)):
        inv_rows[i : i + 1, :] = row
    columns = inv_rows[...].T
    for i in range(len(PAIRS)):
        inv_full[i] = jnp.broadcast_to(columns[:, i : i + 1], (N, BLK))

    for c, (first, count) in enumerate(CHUNKS):
        settle(recv1, rs1.at[c], first, count)
        owns1[c].wait()
        for u in range(first, first + count):
            part = jnp.dot(
                w[u], recv1[u].reshape(N * UNIT, BLK), preferred_element_type=f32
            )
            if u == 0:
                moments[...] = part
            else:
                moments[...] += part

    at = {}
    for i, (k, l) in enumerate(PAIRS):
        at[k, l] = at[l, k] = i

    @pl.loop(0, N // 16)
    def _(i):
        rows = pl.multiple_of(i * 16, 16)
        given = [moments[pl.ds(l * N + rows, 16), :] for l in range(TERMS)]
        for k in range(TERMS):
            value = inv_full[at[k, 0], pl.ds(rows, 16), :] * given[0]
            for l in range(1, TERMS):
                value = value + inv_full[at[k, l], pl.ds(rows, 16), :] * given[l]
            coefs[k, pl.ds(rows, 16), :] = value.astype(bf16)
            ctmp[pl.ds(rows * 8 + k, 16, stride=8), :] = value
        ctmp[pl.ds(rows * 8 + 7, 16, stride=8), :] = jnp.zeros((16, BLK), f32)
        coef_send[pl.ds(rows, 16)] = (
            ctmp[pl.ds(rows * 8, 128), :].astype(bf16).reshape(16, 8, BLK)
        )

    own_coef = pltpu.make_async_copy(coef_send.at[me], coef_recv.at[me], own_sem.at[7])
    own_coef.start()

    @pl.loop(1, N, unroll=4)
    def _(i):
        peer = lax.rem(me + i * 37, N)
        pltpu.make_async_remote_copy(
            src_ref=coef_send.at[peer], dst_ref=coef_recv.at[me],
            send_sem=coef_ss, recv_sem=coef_rs, device_id=(peer,), device_id_type=MESH,
        ).start()

    for k in range(TERMS):
        coefs_t[:, k * N : (k + 1) * N] = coefs[k].T

    def predict(u):
        @pl.loop(0, 4)
        def _(i):
            lanes = pl.ds(pl.multiple_of(i * 512, 512), 512)
            value = jnp.dot(coefs_t[...], w[u, :, lanes], preferred_element_type=f32)
            send2[u, pl.ds(i * 32, 32)] = value.astype(bf16).T.reshape(32, UNIT, BLK)

    owns2 = []
    for c, (first, count) in enumerate(CHUNKS):
        for u in range(first, first + count):
            predict(u)
        owns2.append(exchange(send2, recv2, ss2.at[c], rs2.at[c], first, count, 3 + c))

    @pl.loop(0, UNITS * UNIT, unroll=4)
    def _(p):
        rv[p] = rv[p].T

    part = coef_recv.at[pl.ds(0, N - 1)]
    pltpu.make_async_copy(part, part, coef_rs).wait()
    own_coef.wait()
    ctmp[...] = coef_recv[...].astype(f32).reshape(N * 8, BLK)
    for k in range(TERMS):
        coef_out[k] = ctmp[pl.ds(k, N, stride=8), :]
    outs = [pltpu.make_async_copy(coef_out, coef_hbm, out_sem.at[UNITS])]
    outs[0].start()

    for c, (first, count) in enumerate(CHUNKS):
        settle(recv2, rs2.at[c], first, count)
        owns2[c].wait()
        for u in range(first, first + count):
            @pl.loop(0, 8)
            def _(i):
                rows = recv2[u, pl.ds(i * 16, 16)].astype(f32).reshape(256, BLK)
                tmp[pl.ds(pl.multiple_of(i * 256, 256), 256), :] = rows

            for e in range(UNIT):
                p = u * UNIT + e
                predicted = tmp[pl.ds(e, BLK, stride=UNIT), :].astype(bf16)
                back = jnp.dot(predicted, cv[p], preferred_element_type=f32).astype(bf16)
                adjoint = jnp.dot(rv[p], back, preferred_element_type=f32)
                bv[p] = (bv[p].astype(f32) - adjoint).astype(bf16)
            part = pl.ds(u * UNIT, UNIT)
            outs.append(pltpu.make_async_copy(bv.at[part], res_hbm.at[part], out_sem.at[u]))
            outs[-1].start()

    part = meta.at[pl.ds(0, N - 1)]
    pltpu.make_async_copy(part, part, meta_ss).wait()
    part = coef_send.at[pl.ds(0, N - 1)]
    pltpu.make_async_copy(part, part, coef_ss).wait()
    for c, (first, count) in enumerate(CHUNKS):
        settle(send1, ss1.at[c], first, count)
        settle(send2, ss2.at[c], first, count)
    for copy in outs:
        copy.wait()


def move(coef, res, coef_out, res_out, coef_vmem, res_vmem, sem):
    refs = [(coef, coef_vmem, coef_out)]
    for i in range(MOVES):
        part = pl.ds(i * (UNITS * UNIT // MOVES), UNITS * UNIT // MOVES)
        refs.append((res.at[part], res_vmem.at[part], res_out.at[part]))
    loads = [pltpu.make_async_copy(src, mid, sem.at[0, i]) for i, (src, mid, _) in enumerate(refs)]
    stores = [pltpu.make_async_copy(mid, dst, sem.at[1, i]) for i, (_, mid, dst) in enumerate(refs)]
    for copy in loads:
        copy.start()
    for load, store in zip(loads, stores):
        load.wait()
        store.start()
    for copy in stores:
        copy.wait()


def on_device(blocks, row_maps, col_maps, targets, date_index):
    entries = UNITS * UNIT
    harmonic = harmonic_table()
    table = np.zeros((8, DATES), np.float32)
    table[:TERMS] = harmonic.T
    products = np.zeros((32, DATES), np.float32)
    for i, (k, l) in enumerate(PAIRS):
        products[i] = harmonic[:, k] * harmonic[:, l]
    dma = pltpu.SemaphoreType.DMA
    chunks = len(CHUNKS)
    vmem = pl.BlockSpec(memory_space=pltpu.VMEM)
    hbm = pl.BlockSpec(memory_space=pl.ANY)
    outs = (
        jax.ShapeDtypeStruct((TERMS, BLK, BLK), f32),
        jax.ShapeDtypeStruct((entries, BLK, BLK), bf16),
    )
    coef, res = pl.pallas_call(
        kernel,
        out_shape=outs,
        in_specs=[hbm] * 3 + [vmem] * 4,
        out_specs=(hbm, hbm),
        scratch_shapes=[
            pltpu.VMEM((entries, BLK, BLK), bf16),
            pltpu.VMEM((entries, BLK, BLK), bf16),
            pltpu.VMEM((entries, BLK, BLK), bf16),
            pltpu.VMEM((1, 128), jnp.int32),
            pltpu.VMEM((N, 1, 128), jnp.int32),
            pltpu.VMEM((UNITS, N, UNIT, BLK), bf16),
            pltpu.VMEM((UNITS, N, UNIT, BLK), bf16),
            pltpu.VMEM((UNITS, N, UNIT, BLK), bf16),
            pltpu.VMEM((UNITS, N, UNIT, BLK), bf16),
            pltpu.VMEM((UNITS, TERMS * N, N * UNIT), bf16),
            pltpu.VMEM((N * UNIT, BLK), f32),
            pltpu.VMEM((UNITS * 8, PAIR), f32),
            pltpu.VMEM((UNITS * 8, PAIR), f32),
            pltpu.VMEM((DATES, N), f32),
            pltpu.VMEM((32, N), f32),
            pltpu.VMEM((len(PAIRS), N, BLK), f32),
            pltpu.VMEM((TERMS * N, BLK), f32),
            pltpu.VMEM((BLK, TERMS * N), bf16),
            pltpu.VMEM((TERMS, N, BLK), bf16),
            pltpu.VMEM((N, 8, BLK), bf16),
            pltpu.VMEM((N, 8, BLK), bf16),
            pltpu.VMEM((N * 8, BLK), f32),
            pltpu.VMEM((TERMS, N, BLK), f32),
            dma((3, UNITS)),
            pltpu.SemaphoreType.REGULAR,
            dma,
            dma,
            dma((chunks,)),
            dma((chunks,)),
            dma((chunks,)),
            dma((chunks,)),
            dma,
            dma,
            dma((8,)),
            dma((UNITS + 1,)),
        ],
        compiler_params=pltpu.CompilerParams(
            collective_id=0, has_side_effects=True, vmem_limit_bytes=58 * 2**20
        ),
        name="fit",
    )(
        blocks, row_maps, col_maps, targets.reshape(1, entries), date_index.reshape(1, entries),
        jnp.asarray(table), jnp.asarray(products),
    )
    return pl.pallas_call(
        move,
        out_shape=outs,
        in_specs=[hbm] * 2,
        out_specs=(hbm, hbm),
        scratch_shapes=[
            pltpu.VMEM((TERMS, BLK, BLK), f32),
            pltpu.VMEM((entries, BLK, BLK), bf16),
            dma((2, MOVES + 1)),
        ],
        compiler_params=pltpu.CompilerParams(vmem_limit_bytes=60 * 2**20),
        name="move",
    )(coef, res)


def solution(mesh):
    placed = (
        P("dev", None, None),
        P("dev", None, None),
        P("dev", None, None),
        P("dev", None),
        P("dev"),
    )
    return jax.shard_map(
        on_device,
        mesh=mesh,
        in_specs=placed,
        out_specs=(P("dev", None, None), P("dev", None, None)),
        check_vma=False,
    )
```

```python
import functools

import jax
import jax.numpy as jnp
import numpy as np
from jax import lax
from jax.experimental import pallas as pl
from jax.experimental.pallas import tpu as pltpu
from jax.sharding import PartitionSpec as P

N = 128
DATES = 32
TERMS = 7
BLK = 128
UNIT = 16
UNITS = 4
PAIR = 256
LOW = 16
MOVES = 8
BATCH = 8
CHUNKS = ((0, 1), (1, 2), (3, 1))
MESH = pl.DeviceIdType.MESH
f32 = jnp.float32
bf16 = jnp.bfloat16
highest = lax.Precision.HIGHEST
PAIRS = [(k, l) for k in range(TERMS) for l in range(k + 1)]


def harmonic_table():
    angles = 2.0 * np.pi * np.arange(DATES) / DATES
    columns = [np.ones(DATES)]
    for degree in range(1, 4):
        columns.append(np.cos(degree * angles))
        columns.append(np.sin(degree * angles))
    return np.stack(columns, axis=1)


def iota(shape, dim):
    return lax.broadcasted_iota(jnp.int32, shape, dim)


def inverse_rows(normal):
    low = {}
    for j in range(TERMS):
        for i in range(j, TERMS):
            s = normal[i, j]
            for m in range(j):
                s = s - low[i, m] * low[j, m]
            if i == j:
                root = jnp.sqrt(s)
                low[j, j] = root
                low[j, "inv"] = 1.0 / root
            else:
                low[i, j] = s * low[j, "inv"]
    inv = {}
    for j in range(TERMS):
        inv[j, j] = low[j, "inv"]
        for i in range(j + 1, TERMS):
            s = low[i, j] * inv[j, j]
            for m in range(j + 1, i):
                s = s + low[i, m] * inv[m, j]
            inv[i, j] = -s * low[i, "inv"]
    out = []
    for k, l in PAIRS:
        s = inv[k, k] * inv[k, l]
        for m in range(k + 1, TERMS):
            s = s + inv[m, k] * inv[m, l]
        out.append(s)
    return out


def kernel(
    b_hbm, r_hbm, c_hbm, t_ref, d_ref, table_ref, products_ref,
    coef_hbm, res_hbm,
    bv, rv, cv, meta_own, meta, send1, recv1, send2, recv2, w, tmp,
    trow, drow, tally, inv_rows, inv_full, moments, coefs_t, coefs, coef_send, coef_recv, ctmp,
    load_sem, stage_sem, meta_ss, meta_rs, ss1, rs1, ss2, rs2, coef_ss, coef_rs, own_sem, out_sem,
):
    me = lax.axis_index("dev")
    loads = []
    for u in range(UNITS):
        part = pl.ds(u * UNIT, UNIT)
        loads.append([
            pltpu.make_async_copy(src.at[part], dst.at[part], load_sem.at[i, u])
            for i, (src, dst) in enumerate(((b_hbm, bv), (c_hbm, cv), (r_hbm, rv)))
        ])
    for copy in loads[0]:
        copy.start()

    barrier = pltpu.get_barrier_semaphore()
    base = (me // LOW) * LOW

    @pl.loop(1, LOW)
    def _(i):
        peer = base + lax.rem(me + i, LOW)
        pl.semaphore_signal(barrier, inc=1, device_id=(peer,), device_id_type=MESH)

    @pl.loop(1, N // LOW)
    def _(i):
        peer = lax.rem(me + i * LOW, N)
        pl.semaphore_signal(barrier, inc=1, device_id=(peer,), device_id_type=MESH)

    def greet():
        pl.semaphore_wait(barrier, LOW - 1 + N // LOW - 1)

        @pl.loop(1, N // LOW)
        def _(i):
            peer = lax.rem(me + i * LOW, N)
            pl.semaphore_signal(stage_sem, inc=1, device_id=(peer,), device_id_type=MESH)

    def resample(u):
        for copy in loads[u]:
            copy.wait()
        for e in range(UNIT):
            if u == 0 and e == 0:
                for group in loads[1:]:
                    for copy in group:
                        copy.start()
            if u == 0 and e == UNIT // 2:
                greet()
            if e % BATCH:
                continue
            batch = range(e, e + BATCH)
            halves = [
                lax.dot_general(
                    bv[u * UNIT + i], cv[u * UNIT + i], (((1,), (1,)), ((), ())),
                    preferred_element_type=f32,
                ).astype(bf16)
                for i in batch
            ]
            for i, half in zip(batch, halves):
                tmp[pl.ds(i, BLK, stride=UNIT), :] = jnp.dot(
                    rv[u * UNIT + i], half, preferred_element_type=f32
                )

        @pl.loop(0, 8)
        def _(i):
            rows = tmp[pl.ds(pl.multiple_of(i * 256, 256), 256), :]
            send1[u, pl.ds(i * 16, 16)] = rows.astype(bf16).reshape(16, UNIT, BLK)

    def exchange(src, dst, ss, rs, first, count, lane):
        units = pl.ds(first, count)
        own = pltpu.make_async_copy(src.at[units, me], dst.at[units, me], own_sem.at[lane])
        own.start()

        @pl.loop(1, N, unroll=4)
        def _(i):
            peer = lax.rem(me + i * 37, N)
            pltpu.make_async_remote_copy(
                src_ref=src.at[units, peer], dst_ref=dst.at[units, me],
                send_sem=ss, recv_sem=rs, device_id=(peer,), device_id_type=MESH,
            ).start()

        return own

    def settle(ref, sem, first, count):
        part = ref.at[pl.ds(first, count), pl.ds(0, N - 1)]
        pltpu.make_async_copy(part, part, sem).wait()

    meta_own[0:1, 0:64] = t_ref[...]
    meta_own[0:1, 64:128] = d_ref[...]
    resample(0)
    pl.semaphore_wait(stage_sem, N // LOW - 1)

    owns1 = []
    for c, (first, count) in enumerate(CHUNKS):
        for u in range(first, first + count):
            if u > 0:
                resample(u)
        owns1.append(exchange(send1, recv1, ss1.at[c], rs1.at[c], first, count, c))
        if c == 0:
            own_meta = pltpu.make_async_copy(meta_own, meta.at[me], own_sem.at[6])
            own_meta.start()

            @pl.loop(1, N, unroll=4)
            def _(i):
                peer = lax.rem(me + i * 37, N)
                pltpu.make_async_remote_copy(
                    src_ref=meta_own, dst_ref=meta.at[me],
                    send_sem=meta_ss, recv_sem=meta_rs, device_id=(peer,), device_id_type=MESH,
                ).start()

    part = meta.at[pl.ds(0, N - 1)]
    pltpu.make_async_copy(part, part, meta_rs).wait()
    own_meta.wait()
    names = meta[:, 0, :].astype(f32).astype(bf16)
    lane_in, lane_out = iota((N, PAIR), 0), iota((N, PAIR), 1)
    mine = (lane_out // UNIT) == lax.rem(lane_in, 16)
    gather = (iota((8, N), 0) == iota((8, N), 1) // 16).astype(f32).astype(bf16)
    for u in range(UNITS):
        for start, out in ((0, trow), (64, drow)):
            pick = (lane_in == start + u * UNIT + lax.rem(lane_out, UNIT)).astype(f32).astype(bf16)
            spread = jnp.dot(names, pick, preferred_element_type=f32)
            spread = jnp.where(mine, spread, 0.0).astype(bf16)
            out[pl.ds(u * 8, 8), :] = jnp.dot(gather, spread, preferred_element_type=f32)

    tally[...] = jnp.zeros_like(tally)
    table = table_ref[...].astype(bf16)

    @pl.loop(0, UNITS)
    def _(u):
        @pl.loop(0, 8)
        def _(g):
            pair = u * 8 + g
            tile = trow[pl.ds(pair, 1), :]
            date = drow[pl.ds(pair, 1), :]
            tile_hot = (iota((N, PAIR), 0).astype(f32) == tile).astype(f32).astype(bf16)
            date_hot = (iota((DATES, PAIR), 0).astype(f32) == date).astype(f32).astype(bf16)
            tally[...] += lax.dot_general(
                date_hot, tile_hot, (((1,), (1,)), ((), ())), preferred_element_type=f32
            )
            weights = jnp.dot(table, date_hot, preferred_element_type=f32)
            lanes = pl.ds(pl.multiple_of(g * PAIR, PAIR), PAIR)
            for k in range(TERMS):
                w[u, pl.ds(k * N, N), lanes] = tile_hot * weights[k : k + 1, :].astype(bf16)

    normal_rows = jnp.dot(products_ref[...], tally[...], precision=highest, preferred_element_type=f32)
    normal = {}
    for i, (k, l) in enumerate(PAIRS):
        row = normal_rows[i : i + 1, :]
        normal[k, l] = row + 1.0 if k == l else row
    inv_rows[...] = jnp.zeros_like(inv_rows)
    for i, row in enumerate(inverse_rows(normal)):
        inv_rows[i : i + 1, :] = row
    columns = inv_rows[...].T
    for i in range(len(PAIRS)):
        inv_full[i] = jnp.broadcast_to(columns[:, i : i + 1], (N, BLK))

    for c, (first, count) in enumerate(CHUNKS):
        settle(recv1, rs1.at[c], first, count)
        owns1[c].wait()
        for u in range(first, first + count):
            part = jnp.dot(
                w[u], recv1[u].reshape(N * UNIT, BLK), preferred_element_type=f32
            )
            if u == 0:
                moments[...] = part
            else:
                moments[...] += part

    at = {}
    for i, (k, l) in enumerate(PAIRS):
        at[k, l] = at[l, k] = i

    @pl.loop(0, N // 16)
    def _(i):
        rows = pl.multiple_of(i * 16, 16)
        given = [moments[pl.ds(l * N + rows, 16), :] for l in range(TERMS)]
        for k in range(TERMS):
            value = inv_full[at[k, 0], pl.ds(rows, 16), :] * given[0]
            for l in range(1, TERMS):
                value = value + inv_full[at[k, l], pl.ds(rows, 16), :] * given[l]
            coefs[k, pl.ds(rows, 16), :] = value.astype(bf16)
            ctmp[pl.ds(rows * 8 + k, 16, stride=8), :] = value
        ctmp[pl.ds(rows * 8 + 7, 16, stride=8), :] = jnp.zeros((16, BLK), f32)

    for k in range(TERMS):
        coefs_t[:, k * N : (k + 1) * N] = coefs[k].T

    def predict(u):
        @pl.loop(0, 4)
        def _(i):
            lanes = pl.ds(pl.multiple_of(i * 512, 512), 512)
            value = jnp.dot(coefs_t[...], w[u, :, lanes], preferred_element_type=f32)
            send2[u, pl.ds(i * 32, 32)] = value.astype(bf16).T.reshape(32, UNIT, BLK)

    owns2 = []
    for c, (first, count) in enumerate(CHUNKS):
        for u in range(first, first + count):
            predict(u)
        owns2.append(exchange(send2, recv2, ss2.at[c], rs2.at[c], first, count, 3 + c))

    @pl.loop(0, UNITS * UNIT, unroll=4)
    def _(p):
        rv[p] = rv[p].T

    @pl.loop(0, 8)
    def _(i):
        rows = ctmp[pl.ds(pl.multiple_of(i * 128, 128), 128), :]
        coef_send[pl.ds(i * 16, 16)] = rows.astype(bf16).reshape(16, 8, BLK)

    own_coef = pltpu.make_async_copy(coef_send.at[me], coef_recv.at[me], own_sem.at[7])
    own_coef.start()

    @pl.loop(1, N, unroll=4)
    def _(i):
        peer = lax.rem(me + i * 37, N)
        pltpu.make_async_remote_copy(
            src_ref=coef_send.at[peer], dst_ref=coef_recv.at[me],
            send_sem=coef_ss, recv_sem=coef_rs, device_id=(peer,), device_id_type=MESH,
        ).start()

    outs = []
    for c, (first, count) in enumerate(CHUNKS):
        settle(recv2, rs2.at[c], first, count)
        owns2[c].wait()
        for u in range(first, first + count):
            @pl.loop(0, 8)
            def _(i):
                rows = recv2[u, pl.ds(i * 16, 16)].astype(f32).reshape(256, BLK)
                tmp[pl.ds(pl.multiple_of(i * 256, 256), 256), :] = rows

            for e in range(0, UNIT, BATCH):
                batch = range(e, e + BATCH)
                backs = [
                    jnp.dot(
                        tmp[pl.ds(i, BLK, stride=UNIT), :].astype(bf16), cv[u * UNIT + i],
                        preferred_element_type=f32,
                    ).astype(bf16)
                    for i in batch
                ]
                adjoints = [
                    jnp.dot(rv[u * UNIT + i], back, preferred_element_type=f32)
                    for i, back in zip(batch, backs)
                ]
                for i, adjoint in zip(batch, adjoints):
                    p = u * UNIT + i
                    bv[p] = (bv[p].astype(f32) - adjoint).astype(bf16)
            part = pl.ds(u * UNIT, UNIT)
            outs.append(pltpu.make_async_copy(bv.at[part], res_hbm.at[part], out_sem.at[u]))
            outs[-1].start()

    part = coef_recv.at[pl.ds(0, N - 1)]
    pltpu.make_async_copy(part, part, coef_rs).wait()
    own_coef.wait()
    outs.append(pltpu.make_async_copy(coef_recv, coef_hbm, out_sem.at[UNITS]))
    outs[-1].start()

    part = meta.at[pl.ds(0, N - 1)]
    pltpu.make_async_copy(part, part, meta_ss).wait()
    part = coef_send.at[pl.ds(0, N - 1)]
    pltpu.make_async_copy(part, part, coef_ss).wait()
    for c, (first, count) in enumerate(CHUNKS):
        settle(send1, ss1.at[c], first, count)
        settle(send2, ss2.at[c], first, count)
    for copy in outs:
        copy.wait()


def finish(coef, res, coef_out, res_out, rows, planes, sem):
    stores = []
    for i in range(MOVES):
        part = pl.ds(i * (UNITS * UNIT // MOVES), UNITS * UNIT // MOVES)
        stores.append(pltpu.make_async_copy(res.at[part], res_out.at[part], sem.at[i]))
        stores[-1].start()
    rows[...] = coef[...].astype(f32).reshape(N * 8, BLK)
    for k in range(TERMS):
        planes[k] = rows[pl.ds(k, N, stride=8), :]
    stores.append(pltpu.make_async_copy(planes, coef_out, sem.at[MOVES]))
    stores[-1].start()
    for copy in stores:
        copy.wait()


def on_device(blocks, row_maps, col_maps, targets, date_index):
    entries = UNITS * UNIT
    harmonic = harmonic_table()
    table = np.zeros((8, DATES), np.float32)
    table[:TERMS] = harmonic.T
    products = np.zeros((32, DATES), np.float32)
    for i, (k, l) in enumerate(PAIRS):
        products[i] = harmonic[:, k] * harmonic[:, l]
    dma = pltpu.SemaphoreType.DMA
    chunks = len(CHUNKS)
    vmem = pl.BlockSpec(memory_space=pltpu.VMEM)
    hbm = pl.BlockSpec(memory_space=pl.ANY)
    outs = (
        jax.ShapeDtypeStruct((TERMS, BLK, BLK), f32),
        jax.ShapeDtypeStruct((entries, BLK, BLK), bf16),
    )
    coef, res = pl.pallas_call(
        kernel,
        out_shape=(pltpu.VMEM((N, 8, BLK), bf16), pltpu.VMEM((entries, BLK, BLK), bf16)),
        in_specs=[hbm] * 3 + [vmem] * 4,
        out_specs=(hbm, hbm),
        scratch_shapes=[
            pltpu.VMEM((entries, BLK, BLK), bf16),
            pltpu.VMEM((entries, BLK, BLK), bf16),
            pltpu.VMEM((entries, BLK, BLK), bf16),
            pltpu.VMEM((1, 128), jnp.int32),
            pltpu.VMEM((N, 1, 128), jnp.int32),
            pltpu.VMEM((UNITS, N, UNIT, BLK), bf16),
            pltpu.VMEM((UNITS, N, UNIT, BLK), bf16),
            pltpu.VMEM((UNITS, N, UNIT, BLK), bf16),
            pltpu.VMEM((UNITS, N, UNIT, BLK), bf16),
            pltpu.VMEM((UNITS, TERMS * N, N * UNIT), bf16),
            pltpu.VMEM((N * UNIT, BLK), f32),
            pltpu.VMEM((UNITS * 8, PAIR), f32),
            pltpu.VMEM((UNITS * 8, PAIR), f32),
            pltpu.VMEM((DATES, N), f32),
            pltpu.VMEM((32, N), f32),
            pltpu.VMEM((len(PAIRS), N, BLK), f32),
            pltpu.VMEM((TERMS * N, BLK), f32),
            pltpu.VMEM((BLK, TERMS * N), bf16),
            pltpu.VMEM((TERMS, N, BLK), bf16),
            pltpu.VMEM((N, 8, BLK), bf16),
            pltpu.VMEM((N, 8, BLK), bf16),
            pltpu.VMEM((N * 8, BLK), f32),
            dma((3, UNITS)),
            pltpu.SemaphoreType.REGULAR,
            dma,
            dma,
            dma((chunks,)),
            dma((chunks,)),
            dma((chunks,)),
            dma((chunks,)),
            dma,
            dma,
            dma((8,)),
            dma((UNITS + 1,)),
        ],
        compiler_params=pltpu.CompilerParams(
            collective_id=0, has_side_effects=True, vmem_limit_bytes=52 * 2**20
        ),
        name="fit",
    )(
        *[pltpu.with_memory_space_constraint(x, pltpu.HBM) for x in (blocks, row_maps, col_maps)], targets.reshape(1, entries), date_index.reshape(1, entries),
        jnp.asarray(table), jnp.asarray(products),
    )
    return pl.pallas_call(
        finish,
        out_shape=outs,
        in_specs=[vmem] * 2,
        out_specs=(hbm, hbm),
        scratch_shapes=[
            pltpu.VMEM((N * 8, BLK), f32),
            pltpu.VMEM((TERMS, BLK, BLK), f32),
            dma((MOVES + 1,)),
        ],
        compiler_params=pltpu.CompilerParams(vmem_limit_bytes=16 * 2**20),
        name="finish",
    )(coef, res)


def solution(mesh):
    placed = (
        P("dev", None, None),
        P("dev", None, None),
        P("dev", None, None),
        P("dev", None),
        P("dev"),
    )
    return jax.shard_map(
        on_device,
        mesh=mesh,
        in_specs=placed,
        out_specs=(P("dev", None, None), P("dev", None, None)),
        check_vma=False,
    )
```

```python
import functools

import jax
import jax.numpy as jnp
import numpy as np
from jax import lax
from jax.experimental import pallas as pl
from jax.experimental.pallas import tpu as pltpu
from jax.sharding import PartitionSpec as P

N = 128
DATES = 32
TERMS = 7
BLK = 128
UNIT = 16
UNITS = 4
PAIR = 256
MOVES = 8
BATCH = 8
CHUNKS = ((0, 1), (1, 2), (3, 1))
MESH = pl.DeviceIdType.MESH
f32 = jnp.float32
bf16 = jnp.bfloat16
highest = lax.Precision.HIGHEST
PAIRS = [(k, l) for k in range(TERMS) for l in range(k + 1)]


def harmonic_table():
    angles = 2.0 * np.pi * np.arange(DATES) / DATES
    columns = [np.ones(DATES)]
    for degree in range(1, 4):
        columns.append(np.cos(degree * angles))
        columns.append(np.sin(degree * angles))
    return np.stack(columns, axis=1)


def iota(shape, dim):
    return lax.broadcasted_iota(jnp.int32, shape, dim)


def inverse_rows(normal):
    low = {}
    for j in range(TERMS):
        for i in range(j, TERMS):
            s = normal[i, j]
            for m in range(j):
                s = s - low[i, m] * low[j, m]
            if i == j:
                root = jnp.sqrt(s)
                low[j, j] = root
                low[j, "inv"] = 1.0 / root
            else:
                low[i, j] = s * low[j, "inv"]
    inv = {}
    for j in range(TERMS):
        inv[j, j] = low[j, "inv"]
        for i in range(j + 1, TERMS):
            s = low[i, j] * inv[j, j]
            for m in range(j + 1, i):
                s = s + low[i, m] * inv[m, j]
            inv[i, j] = -s * low[i, "inv"]
    out = []
    for k, l in PAIRS:
        s = inv[k, k] * inv[k, l]
        for m in range(k + 1, TERMS):
            s = s + inv[m, k] * inv[m, l]
        out.append(s)
    return out


def kernel(
    b_hbm, r_hbm, c_hbm, t_ref, d_ref, table_ref, products_ref,
    coef_ref, res_ref,
    bv, rv, cv, meta_own, meta, send1, recv1, send2, recv2, w, tmp,
    trow, drow, tally, inv_rows, inv_full, moments, coefs_t, coefs, coef_send, coef_recv, ctmp,
    load_sem, meta_ss, meta_rs, ss1, rs1, ss2, rs2, coef_ss, coef_rs, own_sem,
):
    me = lax.axis_index("dev")
    loads = []
    for u in range(UNITS):
        part = pl.ds(u * UNIT, UNIT)
        loads.append([
            pltpu.make_async_copy(src.at[part], dst.at[part], load_sem.at[i, u])
            for i, (src, dst) in enumerate(((b_hbm, bv), (c_hbm, cv), (r_hbm, rv)))
        ])
    for copy in loads[0]:
        copy.start()

    barrier = pltpu.get_barrier_semaphore()

    @pl.loop(1, N, unroll=4)
    def _(i):
        peer = lax.rem(me + i * 45, N)
        pl.semaphore_signal(barrier, inc=1, device_id=(peer,), device_id_type=MESH)

    def resample(u):
        for copy in loads[u]:
            copy.wait()
        for e in range(UNIT):
            if u == 0 and e == 0:
                for group in loads[1:]:
                    for copy in group:
                        copy.start()
            if e % BATCH:
                continue
            batch = range(e, e + BATCH)
            halves = [
                lax.dot_general(
                    bv[u * UNIT + i], cv[u * UNIT + i], (((1,), (1,)), ((), ())),
                    preferred_element_type=f32,
                ).astype(bf16)
                for i in batch
            ]
            for i, half in zip(batch, halves):
                tmp[pl.ds(i, BLK, stride=UNIT), :] = jnp.dot(
                    rv[u * UNIT + i], half, preferred_element_type=f32
                )

        @pl.loop(0, 8, unroll=8)
        def _(i):
            rows = tmp[pl.ds(pl.multiple_of(i * 256, 256), 256), :]
            send1[u, pl.ds(i * 16, 16)] = rows.astype(bf16).reshape(16, UNIT, BLK)

    def exchange(src, dst, ss, rs, first, count, lane):
        units = pl.ds(first, count)
        own = pltpu.make_async_copy(src.at[units, me], dst.at[units, me], own_sem.at[lane])
        own.start()

        @pl.loop(1, N, unroll=4)
        def _(i):
            peer = lax.rem(me + i * 45, N)
            pltpu.make_async_remote_copy(
                src_ref=src.at[units, peer], dst_ref=dst.at[units, me],
                send_sem=ss, recv_sem=rs, device_id=(peer,), device_id_type=MESH,
            ).start()

        return own

    def settle(ref, sem, first, count):
        part = ref.at[pl.ds(first, count), pl.ds(0, N - 1)]
        pltpu.make_async_copy(part, part, sem).wait()

    meta_own[0:1, 0:64] = t_ref[...]
    meta_own[0:1, 64:128] = d_ref[...]
    resample(0)
    pl.semaphore_wait(barrier, N - 1)

    owns1 = []
    for c, (first, count) in enumerate(CHUNKS):
        for u in range(first, first + count):
            if u > 0:
                resample(u)
        owns1.append(exchange(send1, recv1, ss1.at[c], rs1.at[c], first, count, c))
        if c == 0:
            own_meta = pltpu.make_async_copy(meta_own, meta.at[me], own_sem.at[6])
            own_meta.start()

            @pl.loop(1, N, unroll=4)
            def _(i):
                peer = lax.rem(me + i * 45, N)
                pltpu.make_async_remote_copy(
                    src_ref=meta_own, dst_ref=meta.at[me],
                    send_sem=meta_ss, recv_sem=meta_rs, device_id=(peer,), device_id_type=MESH,
                ).start()

    part = meta.at[pl.ds(0, N - 1)]
    pltpu.make_async_copy(part, part, meta_rs).wait()
    own_meta.wait()
    names = meta[:, 0, :].astype(f32).astype(bf16)
    lane_in, lane_out = iota((N, PAIR), 0), iota((N, PAIR), 1)
    mine = (lane_out // UNIT) == lax.rem(lane_in, 16)
    gather = (iota((8, N), 0) == iota((8, N), 1) // 16).astype(f32).astype(bf16)
    for u in range(UNITS):
        for start, out in ((0, trow), (64, drow)):
            pick = (lane_in == start + u * UNIT + lax.rem(lane_out, UNIT)).astype(f32).astype(bf16)
            spread = jnp.dot(names, pick, preferred_element_type=f32)
            spread = jnp.where(mine, spread, 0.0).astype(bf16)
            out[pl.ds(u * 8, 8), :] = jnp.dot(gather, spread, preferred_element_type=f32)

    tally[...] = jnp.zeros_like(tally)
    table = table_ref[...].astype(bf16)

    @pl.loop(0, UNITS)
    def _(u):
        @pl.loop(0, 8, unroll=2)
        def _(g):
            pair = u * 8 + g
            tile = trow[pl.ds(pair, 1), :]
            date = drow[pl.ds(pair, 1), :]
            tile_hot = (iota((N, PAIR), 0).astype(f32) == tile).astype(f32).astype(bf16)
            date_hot = (iota((DATES, PAIR), 0).astype(f32) == date).astype(f32).astype(bf16)
            tally[...] += lax.dot_general(
                date_hot, tile_hot, (((1,), (1,)), ((), ())), preferred_element_type=f32
            )
            weights = jnp.dot(table, date_hot, preferred_element_type=f32)
            lanes = pl.ds(pl.multiple_of(g * PAIR, PAIR), PAIR)
            for k in range(TERMS):
                w[u, pl.ds(k * N, N), lanes] = tile_hot * weights[k : k + 1, :].astype(bf16)

    normal_rows = jnp.dot(products_ref[...], tally[...], precision=highest, preferred_element_type=f32)
    normal = {}
    for i, (k, l) in enumerate(PAIRS):
        row = normal_rows[i : i + 1, :]
        normal[k, l] = row + 1.0 if k == l else row
    inv_rows[...] = jnp.zeros_like(inv_rows)
    for i, row in enumerate(inverse_rows(normal)):
        inv_rows[i : i + 1, :] = row
    columns = inv_rows[...].T
    for i in range(len(PAIRS)):
        inv_full[i] = jnp.broadcast_to(columns[:, i : i + 1], (N, BLK))

    for c, (first, count) in enumerate(CHUNKS):
        settle(recv1, rs1.at[c], first, count)
        owns1[c].wait()
        for u in range(first, first + count):
            part = jnp.dot(
                w[u], recv1[u].reshape(N * UNIT, BLK), preferred_element_type=f32
            )
            if u == 0:
                moments[...] = part
            else:
                moments[...] += part

    at = {}
    for i, (k, l) in enumerate(PAIRS):
        at[k, l] = at[l, k] = i

    @pl.loop(0, N // 16, unroll=2)
    def _(i):
        rows = pl.multiple_of(i * 16, 16)
        given = [moments[pl.ds(l * N + rows, 16), :] for l in range(TERMS)]
        for k in range(TERMS):
            value = inv_full[at[k, 0], pl.ds(rows, 16), :] * given[0]
            for l in range(1, TERMS):
                value = value + inv_full[at[k, l], pl.ds(rows, 16), :] * given[l]
            coefs[k, pl.ds(rows, 16), :] = value.astype(bf16)
            ctmp[pl.ds(rows * 8 + k, 16, stride=8), :] = value
        ctmp[pl.ds(rows * 8 + 7, 16, stride=8), :] = jnp.zeros((16, BLK), f32)

    for k in range(TERMS):
        coefs_t[:, k * N : (k + 1) * N] = coefs[k].T

    def predict(u):
        @pl.loop(0, 4, unroll=4)
        def _(i):
            lanes = pl.ds(pl.multiple_of(i * 512, 512), 512)
            value = jnp.dot(coefs_t[...], w[u, :, lanes], preferred_element_type=f32)
            send2[u, pl.ds(i * 32, 32)] = value.astype(bf16).T.reshape(32, UNIT, BLK)

    owns2 = []
    for c, (first, count) in enumerate(CHUNKS):
        for u in range(first, first + count):
            predict(u)
        owns2.append(exchange(send2, recv2, ss2.at[c], rs2.at[c], first, count, 3 + c))

    @pl.loop(0, UNITS * UNIT, unroll=4)
    def _(p):
        rv[p] = rv[p].T

    @pl.loop(0, 8)
    def _(i):
        rows = ctmp[pl.ds(pl.multiple_of(i * 128, 128), 128), :]
        coef_send[pl.ds(i * 16, 16)] = rows.astype(bf16).reshape(16, 8, BLK)

    own_coef = pltpu.make_async_copy(coef_send.at[me], coef_recv.at[me], own_sem.at[7])
    own_coef.start()

    @pl.loop(1, N, unroll=4)
    def _(i):
        peer = lax.rem(me + i * 45, N)
        pltpu.make_async_remote_copy(
            src_ref=coef_send.at[peer], dst_ref=coef_recv.at[me],
            send_sem=coef_ss, recv_sem=coef_rs, device_id=(peer,), device_id_type=MESH,
        ).start()

    for c, (first, count) in enumerate(CHUNKS):
        settle(recv2, rs2.at[c], first, count)
        owns2[c].wait()
        for u in range(first, first + count):
            @pl.loop(0, 8, unroll=8)
            def _(i):
                rows = recv2[u, pl.ds(i * 16, 16)].astype(f32).reshape(256, BLK)
                tmp[pl.ds(pl.multiple_of(i * 256, 256), 256), :] = rows

            for e in range(0, UNIT, BATCH):
                batch = range(e, e + BATCH)
                backs = [
                    jnp.dot(
                        tmp[pl.ds(i, BLK, stride=UNIT), :].astype(bf16), cv[u * UNIT + i],
                        preferred_element_type=f32,
                    ).astype(bf16)
                    for i in batch
                ]
                adjoints = [
                    jnp.dot(rv[u * UNIT + i], back, preferred_element_type=f32)
                    for i, back in zip(batch, backs)
                ]
                for i, adjoint in zip(batch, adjoints):
                    p = u * UNIT + i
                    res_ref[p] = (bv[p].astype(f32) - adjoint).astype(bf16)

    part = coef_recv.at[pl.ds(0, N - 1)]
    pltpu.make_async_copy(part, part, coef_rs).wait()
    own_coef.wait()
    coef_ref[...] = coef_recv[...]

    part = meta.at[pl.ds(0, N - 1)]
    pltpu.make_async_copy(part, part, meta_ss).wait()
    part = coef_send.at[pl.ds(0, N - 1)]
    pltpu.make_async_copy(part, part, coef_ss).wait()
    for c, (first, count) in enumerate(CHUNKS):
        settle(send1, ss1.at[c], first, count)
        settle(send2, ss2.at[c], first, count)


def finish(coef, res, coef_out, res_out, rows, planes, sem):
    stores = []
    for i in range(MOVES):
        part = pl.ds(i * (UNITS * UNIT // MOVES), UNITS * UNIT // MOVES)
        stores.append(pltpu.make_async_copy(res.at[part], res_out.at[part], sem.at[i]))
        stores[-1].start()
    rows[...] = coef[...].astype(f32).reshape(N * 8, BLK)
    for k in range(TERMS):
        planes[k] = rows[pl.ds(k, N, stride=8), :]
    stores.append(pltpu.make_async_copy(planes, coef_out, sem.at[MOVES]))
    stores[-1].start()
    for copy in stores:
        copy.wait()


def on_device(blocks, row_maps, col_maps, targets, date_index):
    entries = UNITS * UNIT
    harmonic = harmonic_table()
    table = np.zeros((8, DATES), np.float32)
    table[:TERMS] = harmonic.T
    products = np.zeros((32, DATES), np.float32)
    for i, (k, l) in enumerate(PAIRS):
        products[i] = harmonic[:, k] * harmonic[:, l]
    dma = pltpu.SemaphoreType.DMA
    chunks = len(CHUNKS)
    vmem = pl.BlockSpec(memory_space=pltpu.VMEM)
    hbm = pl.BlockSpec(memory_space=pl.ANY)
    outs = (
        jax.ShapeDtypeStruct((TERMS, BLK, BLK), f32),
        jax.ShapeDtypeStruct((entries, BLK, BLK), bf16),
    )
    coef, res = pl.pallas_call(
        kernel,
        out_shape=(pltpu.VMEM((N, 8, BLK), bf16), pltpu.VMEM((entries, BLK, BLK), bf16)),
        in_specs=[hbm] * 3 + [vmem] * 4,
        out_specs=(vmem, vmem),
        scratch_shapes=[
            pltpu.VMEM((entries, BLK, BLK), bf16),
            pltpu.VMEM((entries, BLK, BLK), bf16),
            pltpu.VMEM((entries, BLK, BLK), bf16),
            pltpu.VMEM((1, 128), jnp.int32),
            pltpu.VMEM((N, 1, 128), jnp.int32),
            pltpu.VMEM((UNITS, N, UNIT, BLK), bf16),
            pltpu.VMEM((UNITS, N, UNIT, BLK), bf16),
            pltpu.VMEM((UNITS, N, UNIT, BLK), bf16),
            pltpu.VMEM((UNITS, N, UNIT, BLK), bf16),
            pltpu.VMEM((UNITS, TERMS * N, N * UNIT), bf16),
            pltpu.VMEM((N * UNIT, BLK), f32),
            pltpu.VMEM((UNITS * 8, PAIR), f32),
            pltpu.VMEM((UNITS * 8, PAIR), f32),
            pltpu.VMEM((DATES, N), f32),
            pltpu.VMEM((32, N), f32),
            pltpu.VMEM((len(PAIRS), N, BLK), f32),
            pltpu.VMEM((TERMS * N, BLK), f32),
            pltpu.VMEM((BLK, TERMS * N), bf16),
            pltpu.VMEM((TERMS, N, BLK), bf16),
            pltpu.VMEM((N, 8, BLK), bf16),
            pltpu.VMEM((N, 8, BLK), bf16),
            pltpu.VMEM((N * 8, BLK), f32),
            dma((3, UNITS)),
            dma,
            dma,
            dma((chunks,)),
            dma((chunks,)),
            dma((chunks,)),
            dma((chunks,)),
            dma,
            dma,
            dma((8,)),
        ],
        compiler_params=pltpu.CompilerParams(
            collective_id=0, has_side_effects=True, vmem_limit_bytes=52 * 2**20
        ),
        name="fit",
    )(
        *[pltpu.with_memory_space_constraint(x, pltpu.HBM) for x in (blocks, row_maps, col_maps)], targets.reshape(1, entries), date_index.reshape(1, entries),
        jnp.asarray(table), jnp.asarray(products),
    )
    return pl.pallas_call(
        finish,
        out_shape=outs,
        in_specs=[vmem] * 2,
        out_specs=(hbm, hbm),
        scratch_shapes=[
            pltpu.VMEM((N * 8, BLK), f32),
            pltpu.VMEM((TERMS, BLK, BLK), f32),
            dma((MOVES + 1,)),
        ],
        compiler_params=pltpu.CompilerParams(vmem_limit_bytes=16 * 2**20),
        name="finish",
    )(coef, res)


def solution(mesh):
    placed = (
        P("dev", None, None),
        P("dev", None, None),
        P("dev", None, None),
        P("dev", None),
        P("dev"),
    )
    return jax.shard_map(
        on_device,
        mesh=mesh,
        in_specs=placed,
        out_specs=(P("dev", None, None), P("dev", None, None)),
        check_vma=False,
    )
```

```python
import functools

import jax
import jax.numpy as jnp
import numpy as np
from jax import lax
from jax.experimental import pallas as pl
from jax.experimental.pallas import tpu as pltpu
from jax.sharding import PartitionSpec as P

N = 128
DATES = 32
TERMS = 7
BLK = 128
UNIT = 16
UNITS = 4
PAIR = 256
MOVES = 8
BATCH = 16
CHUNKS = ((0, 1), (1, 2), (3, 1))
MESH = pl.DeviceIdType.MESH
f32 = jnp.float32
bf16 = jnp.bfloat16
highest = lax.Precision.HIGHEST
PAIRS = [(k, l) for k in range(TERMS) for l in range(k + 1)]


def harmonic_table():
    angles = 2.0 * np.pi * np.arange(DATES) / DATES
    columns = [np.ones(DATES)]
    for degree in range(1, 4):
        columns.append(np.cos(degree * angles))
        columns.append(np.sin(degree * angles))
    return np.stack(columns, axis=1)


def iota(shape, dim):
    return lax.broadcasted_iota(jnp.int32, shape, dim)


def inverse_rows(normal):
    low = {}
    for j in range(TERMS):
        for i in range(j, TERMS):
            s = normal[i, j]
            for m in range(j):
                s = s - low[i, m] * low[j, m]
            if i == j:
                root = jnp.sqrt(s)
                low[j, j] = root
                low[j, "inv"] = 1.0 / root
            else:
                low[i, j] = s * low[j, "inv"]
    inv = {}
    for j in range(TERMS):
        inv[j, j] = low[j, "inv"]
        for i in range(j + 1, TERMS):
            s = low[i, j] * inv[j, j]
            for m in range(j + 1, i):
                s = s + low[i, m] * inv[m, j]
            inv[i, j] = -s * low[i, "inv"]
    out = []
    for k, l in PAIRS:
        s = inv[k, k] * inv[k, l]
        for m in range(k + 1, TERMS):
            s = s + inv[m, k] * inv[m, l]
        out.append(s)
    return out


def kernel(
    b_hbm, r_hbm, c_hbm, t_ref, d_ref, table_ref, products_ref,
    coef_ref, res_ref,
    bv, rv, cv, meta_own, meta, send1, recv1, send2, recv2, w, tmp,
    trow, drow, tally, inv_rows, inv_full, moments, coefs_t, coefs, coef_send, coef_recv, ctmp,
    load_sem, meta_ss, meta_rs, ss1, rs1, ss2, rs2, coef_ss, coef_rs, own_sem,
):
    me = lax.axis_index("dev")
    loads = []
    for u in range(UNITS):
        part = pl.ds(u * UNIT, UNIT)
        loads.append([
            pltpu.make_async_copy(src.at[part], dst.at[part], load_sem.at[i, u])
            for i, (src, dst) in enumerate(((b_hbm, bv), (c_hbm, cv), (r_hbm, rv)))
        ])
    for copy in loads[0]:
        copy.start()

    barrier = pltpu.get_barrier_semaphore()

    @pl.loop(1, N, unroll=4)
    def _(i):
        peer = lax.rem(me + i * 45, N)
        pl.semaphore_signal(barrier, inc=1, device_id=(peer,), device_id_type=MESH)

    def resample(u):
        for copy in loads[u]:
            copy.wait()
        for e in range(UNIT):
            if u == 0 and e == 0:
                for group in loads[1:]:
                    for copy in group:
                        copy.start()
            if e % BATCH:
                continue
            batch = range(e, e + BATCH)
            halves = [
                lax.dot_general(
                    bv[u * UNIT + i], cv[u * UNIT + i], (((1,), (1,)), ((), ())),
                    preferred_element_type=f32,
                ).astype(bf16)
                for i in batch
            ]
            for i, half in zip(batch, halves):
                tmp[pl.ds(i, BLK, stride=UNIT), :] = jnp.dot(
                    rv[u * UNIT + i], half, preferred_element_type=f32
                )

        @pl.loop(0, 8, unroll=8)
        def _(i):
            rows = tmp[pl.ds(pl.multiple_of(i * 256, 256), 256), :]
            send1[u, pl.ds(i * 16, 16)] = rows.astype(bf16).reshape(16, UNIT, BLK)

    def exchange(src, dst, ss, rs, first, count, lane):
        units = pl.ds(first, count)
        own = pltpu.make_async_copy(src.at[units, me], dst.at[units, me], own_sem.at[lane])
        own.start()

        @pl.loop(1, N, unroll=4)
        def _(i):
            peer = lax.rem(me + i * 45, N)
            pltpu.make_async_remote_copy(
                src_ref=src.at[units, peer], dst_ref=dst.at[units, me],
                send_sem=ss, recv_sem=rs, device_id=(peer,), device_id_type=MESH,
            ).start()

        return own

    def settle(ref, sem, first, count):
        part = ref.at[pl.ds(first, count), pl.ds(0, N - 1)]
        pltpu.make_async_copy(part, part, sem).wait()

    meta_own[0:1, 0:64] = t_ref[...]
    meta_own[0:1, 64:128] = d_ref[...]
    resample(0)
    pl.semaphore_wait(barrier, N - 1)

    owns1 = []
    for c, (first, count) in enumerate(CHUNKS):
        for u in range(first, first + count):
            if u > 0:
                resample(u)
        owns1.append(exchange(send1, recv1, ss1.at[c], rs1.at[c], first, count, c))
        if c == 0:
            own_meta = pltpu.make_async_copy(meta_own, meta.at[me], own_sem.at[6])
            own_meta.start()

            @pl.loop(1, N, unroll=4)
            def _(i):
                peer = lax.rem(me + i * 45, N)
                pltpu.make_async_remote_copy(
                    src_ref=meta_own, dst_ref=meta.at[me],
                    send_sem=meta_ss, recv_sem=meta_rs, device_id=(peer,), device_id_type=MESH,
                ).start()

    part = meta.at[pl.ds(0, N - 1)]
    pltpu.make_async_copy(part, part, meta_rs).wait()
    own_meta.wait()
    names = meta[:, 0, :].astype(f32).astype(bf16)
    lane_in, lane_out = iota((N, PAIR), 0), iota((N, PAIR), 1)
    mine = (lane_out // UNIT) == lax.rem(lane_in, 16)
    gather = (iota((8, N), 0) == iota((8, N), 1) // 16).astype(f32).astype(bf16)
    for u in range(UNITS):
        for start, out in ((0, trow), (64, drow)):
            pick = (lane_in == start + u * UNIT + lax.rem(lane_out, UNIT)).astype(f32).astype(bf16)
            spread = jnp.dot(names, pick, preferred_element_type=f32)
            spread = jnp.where(mine, spread, 0.0).astype(bf16)
            out[pl.ds(u * 8, 8), :] = jnp.dot(gather, spread, preferred_element_type=f32)

    tally[...] = jnp.zeros_like(tally)
    table = table_ref[...].astype(bf16)

    @pl.loop(0, UNITS)
    def _(u):
        @pl.loop(0, 8, unroll=2)
        def _(g):
            pair = u * 8 + g
            tile = trow[pl.ds(pair, 1), :]
            date = drow[pl.ds(pair, 1), :]
            tile_hot = (iota((N, PAIR), 0).astype(f32) == tile).astype(f32).astype(bf16)
            date_hot = (iota((DATES, PAIR), 0).astype(f32) == date).astype(f32).astype(bf16)
            tally[...] += lax.dot_general(
                date_hot, tile_hot, (((1,), (1,)), ((), ())), preferred_element_type=f32
            )
            weights = jnp.dot(table, date_hot, preferred_element_type=f32)
            lanes = pl.ds(pl.multiple_of(g * PAIR, PAIR), PAIR)
            for k in range(TERMS):
                w[u, pl.ds(k * N, N), lanes] = tile_hot * weights[k : k + 1, :].astype(bf16)

    normal_rows = jnp.dot(products_ref[...], tally[...], precision=highest, preferred_element_type=f32)
    normal = {}
    for i, (k, l) in enumerate(PAIRS):
        row = normal_rows[i : i + 1, :]
        normal[k, l] = row + 1.0 if k == l else row
    inv_rows[...] = jnp.zeros_like(inv_rows)
    for i, row in enumerate(inverse_rows(normal)):
        inv_rows[i : i + 1, :] = row
    columns = inv_rows[...].T
    for i in range(len(PAIRS)):
        inv_full[i] = jnp.broadcast_to(columns[:, i : i + 1], (N, BLK))

    for c, (first, count) in enumerate(CHUNKS):
        settle(recv1, rs1.at[c], first, count)
        owns1[c].wait()
        for u in range(first, first + count):
            part = jnp.dot(
                w[u], recv1[u].reshape(N * UNIT, BLK), preferred_element_type=f32
            )
            if u == 0:
                moments[...] = part
            else:
                moments[...] += part

    at = {}
    for i, (k, l) in enumerate(PAIRS):
        at[k, l] = at[l, k] = i

    @pl.loop(0, N // 16, unroll=2)
    def _(i):
        rows = pl.multiple_of(i * 16, 16)
        given = [moments[pl.ds(l * N + rows, 16), :] for l in range(TERMS)]
        for k in range(TERMS):
            value = inv_full[at[k, 0], pl.ds(rows, 16), :] * given[0]
            for l in range(1, TERMS):
                value = value + inv_full[at[k, l], pl.ds(rows, 16), :] * given[l]
            coefs[k, pl.ds(rows, 16), :] = value.astype(bf16)
            ctmp[pl.ds(rows * 8 + k, 16, stride=8), :] = value
        ctmp[pl.ds(rows * 8 + 7, 16, stride=8), :] = jnp.zeros((16, BLK), f32)

    for k in range(TERMS):
        coefs_t[:, k * N : (k + 1) * N] = coefs[k].T

    def predict(u):
        @pl.loop(0, 4, unroll=4)
        def _(i):
            lanes = pl.ds(pl.multiple_of(i * 512, 512), 512)
            value = jnp.dot(coefs_t[...], w[u, :, lanes], preferred_element_type=f32)
            send2[u, pl.ds(i * 32, 32)] = value.astype(bf16).T.reshape(32, UNIT, BLK)

    owns2 = []
    for c, (first, count) in enumerate(CHUNKS):
        for u in range(first, first + count):
            predict(u)
        owns2.append(exchange(send2, recv2, ss2.at[c], rs2.at[c], first, count, 3 + c))

    @pl.loop(0, UNITS * UNIT, unroll=4)
    def _(p):
        rv[p] = rv[p].T

    @pl.loop(0, 8)
    def _(i):
        rows = ctmp[pl.ds(pl.multiple_of(i * 128, 128), 128), :]
        coef_send[pl.ds(i * 16, 16)] = rows.astype(bf16).reshape(16, 8, BLK)

    own_coef = pltpu.make_async_copy(coef_send.at[me], coef_recv.at[me], own_sem.at[7])
    own_coef.start()

    @pl.loop(1, N, unroll=4)
    def _(i):
        peer = lax.rem(me + i * 45, N)
        pltpu.make_async_remote_copy(
            src_ref=coef_send.at[peer], dst_ref=coef_recv.at[me],
            send_sem=coef_ss, recv_sem=coef_rs, device_id=(peer,), device_id_type=MESH,
        ).start()

    for c, (first, count) in enumerate(CHUNKS):
        settle(recv2, rs2.at[c], first, count)
        owns2[c].wait()
        for u in range(first, first + count):
            @pl.loop(0, 8, unroll=8)
            def _(i):
                rows = recv2[u, pl.ds(i * 16, 16)].astype(f32).reshape(256, BLK)
                tmp[pl.ds(pl.multiple_of(i * 256, 256), 256), :] = rows

            for e in range(0, UNIT, BATCH):
                batch = range(e, e + BATCH)
                backs = [
                    jnp.dot(
                        tmp[pl.ds(i, BLK, stride=UNIT), :].astype(bf16), cv[u * UNIT + i],
                        preferred_element_type=f32,
                    ).astype(bf16)
                    for i in batch
                ]
                adjoints = [
                    jnp.dot(rv[u * UNIT + i], back, preferred_element_type=f32)
                    for i, back in zip(batch, backs)
                ]
                for i, adjoint in zip(batch, adjoints):
                    p = u * UNIT + i
                    res_ref[p] = (bv[p].astype(f32) - adjoint).astype(bf16)

    part = coef_recv.at[pl.ds(0, N - 1)]
    pltpu.make_async_copy(part, part, coef_rs).wait()
    own_coef.wait()
    coef_ref[...] = coef_recv[...]

    part = meta.at[pl.ds(0, N - 1)]
    pltpu.make_async_copy(part, part, meta_ss).wait()
    part = coef_send.at[pl.ds(0, N - 1)]
    pltpu.make_async_copy(part, part, coef_ss).wait()
    for c, (first, count) in enumerate(CHUNKS):
        settle(send1, ss1.at[c], first, count)
        settle(send2, ss2.at[c], first, count)


def finish(coef, res, coef_out, res_out, rows, planes, sem):
    stores = []
    for i in range(MOVES):
        part = pl.ds(i * (UNITS * UNIT // MOVES), UNITS * UNIT // MOVES)
        stores.append(pltpu.make_async_copy(res.at[part], res_out.at[part], sem.at[i]))
        stores[-1].start()
    rows[...] = coef[...].astype(f32).reshape(N * 8, BLK)
    for k in range(TERMS):
        planes[k] = rows[pl.ds(k, N, stride=8), :]
    stores.append(pltpu.make_async_copy(planes, coef_out, sem.at[MOVES]))
    stores[-1].start()
    for copy in stores:
        copy.wait()


def on_device(blocks, row_maps, col_maps, targets, date_index):
    entries = UNITS * UNIT
    harmonic = harmonic_table()
    table = np.zeros((8, DATES), np.float32)
    table[:TERMS] = harmonic.T
    products = np.zeros((32, DATES), np.float32)
    for i, (k, l) in enumerate(PAIRS):
        products[i] = harmonic[:, k] * harmonic[:, l]
    dma = pltpu.SemaphoreType.DMA
    chunks = len(CHUNKS)
    vmem = pl.BlockSpec(memory_space=pltpu.VMEM)
    hbm = pl.BlockSpec(memory_space=pl.ANY)
    outs = (
        jax.ShapeDtypeStruct((TERMS, BLK, BLK), f32),
        jax.ShapeDtypeStruct((entries, BLK, BLK), bf16),
    )
    coef, res = pl.pallas_call(
        kernel,
        out_shape=(pltpu.VMEM((N, 8, BLK), bf16), pltpu.VMEM((entries, BLK, BLK), bf16)),
        in_specs=[hbm] * 3 + [vmem] * 4,
        out_specs=(vmem, vmem),
        scratch_shapes=[
            pltpu.VMEM((entries, BLK, BLK), bf16),
            pltpu.VMEM((entries, BLK, BLK), bf16),
            pltpu.VMEM((entries, BLK, BLK), bf16),
            pltpu.VMEM((1, 128), jnp.int32),
            pltpu.VMEM((N, 1, 128), jnp.int32),
            pltpu.VMEM((UNITS, N, UNIT, BLK), bf16),
            pltpu.VMEM((UNITS, N, UNIT, BLK), bf16),
            pltpu.VMEM((UNITS, N, UNIT, BLK), bf16),
            pltpu.VMEM((UNITS, N, UNIT, BLK), bf16),
            pltpu.VMEM((UNITS, TERMS * N, N * UNIT), bf16),
            pltpu.VMEM((N * UNIT, BLK), f32),
            pltpu.VMEM((UNITS * 8, PAIR), f32),
            pltpu.VMEM((UNITS * 8, PAIR), f32),
            pltpu.VMEM((DATES, N), f32),
            pltpu.VMEM((32, N), f32),
            pltpu.VMEM((len(PAIRS), N, BLK), f32),
            pltpu.VMEM((TERMS * N, BLK), f32),
            pltpu.VMEM((BLK, TERMS * N), bf16),
            pltpu.VMEM((TERMS, N, BLK), bf16),
            pltpu.VMEM((N, 8, BLK), bf16),
            pltpu.VMEM((N, 8, BLK), bf16),
            pltpu.VMEM((N * 8, BLK), f32),
            dma((3, UNITS)),
            dma,
            dma,
            dma((chunks,)),
            dma((chunks,)),
            dma((chunks,)),
            dma((chunks,)),
            dma,
            dma,
            dma((8,)),
        ],
        compiler_params=pltpu.CompilerParams(
            collective_id=0, has_side_effects=True, vmem_limit_bytes=52 * 2**20
        ),
        name="fit",
    )(
        *[pltpu.with_memory_space_constraint(x, pltpu.HBM) for x in (blocks, row_maps, col_maps)], targets.reshape(1, entries), date_index.reshape(1, entries),
        jnp.asarray(table), jnp.asarray(products),
    )
    return pl.pallas_call(
        finish,
        out_shape=outs,
        in_specs=[vmem] * 2,
        out_specs=(hbm, hbm),
        scratch_shapes=[
            pltpu.VMEM((N * 8, BLK), f32),
            pltpu.VMEM((TERMS, BLK, BLK), f32),
            dma((MOVES + 1,)),
        ],
        compiler_params=pltpu.CompilerParams(vmem_limit_bytes=16 * 2**20),
        name="finish",
    )(coef, res)


def solution(mesh):
    placed = (
        P("dev", None, None),
        P("dev", None, None),
        P("dev", None, None),
        P("dev", None),
        P("dev"),
    )
    return jax.shard_map(
        on_device,
        mesh=mesh,
        in_specs=placed,
        out_specs=(P("dev", None, None), P("dev", None, None)),
        check_vma=False,
    )
```
